128 devices in a mesh: space: 64 (over z, x, y_lo, core), samp: 2 (over y_hi).
Axes of the slice: x: 4, y: 4 (y_hi: 2, y_lo: 2; y = y_hi * 2 + y_lo), z: 4, core: 2. Of those that a mesh axis runs over, the one named last changes fastest.
Arguments:
- features: bfloat16 [2, 32, 128, 128, 128], P('samp', None, 'space'), may hold values from -6 to 6
- pre_act: bfloat16 [2, 32, 128, 128, 128], P('samp', None, 'space'), may hold values from -8 to 8
- cotangent: bfloat16 [2, 32, 128, 128, 128], P('samp', None, 'space'), may hold values from -6 to 6
- mix_weight: bfloat16 [32, 32], replicated, may hold values from -1 to 1
- spec_weight: float32 [2, 32, 1024, 32, 32], P(None, None, 'space'), may hold values from -3 to 3
Outputs:
- grad_field: bfloat16 [2, 32, 128, 128, 128], P('samp', None, 'space')
- grad_spec: float32 [2, 32, 1024, 32, 32], P(None, None, ('space', 'samp'))
The draws below stay inside these ranges and needn't reach their ends.
All inputs are finite; a program needn't handle non-finite values.
Results may differ from the reference program's by a relative error of at most 0.0052.
Values sent between devices are 32-bit elements; how exact they have to be, the bound alone decides.
A program may use at most 576 MiB of HBM per device.

```python
import math
import jax
import jax.numpy as jnp
from jax import lax

C = 32
M = 32
G = 128
NX = 128
SAMPLES = 2
PAIRS = 1024


def level_of(own_key, shape, cuts, low, top_value):
    factor_of = 1.0
    for axis_at, parts in cuts:
        draws = jax.random.uniform(jax.random.fold_in(jax.random.fold_in(own_key, 6), axis_at), (parts,), jnp.float32, low / len(cuts), top_value / len(cuts))
        factor_of = factor_of * jnp.repeat(jnp.exp(draws), shape[axis_at] // parts).reshape((-1,) + (1,) * (len(shape) - 1 - axis_at))
    return factor_of


def centred(stream_key, shape, scale, limit, shards=(), held_as=jnp.bfloat16):
    values = scale * jax.random.normal(stream_key, shape, jnp.float32)
    if shards:
        values = values * level_of(stream_key, shape, shards, -0.22, 0.18)
    return jnp.clip(values, -limit, limit).astype(held_as)


def setup_inputs(seed: int = 0) -> dict:
    splits = jax.random.split(jax.random.key(seed), 6)
    features = centred(splits[0], (SAMPLES, C, NX, G, G), 1.0, 6.0, ((0, 2), (2, 64)))
    pre_act = centred(splits[1], (SAMPLES, C, NX, G, G), 1.5, 8.0, ((0, 2), (2, 64)))
    cotangent = centred(splits[2], (SAMPLES, C, NX, G, G), 1.0, 6.0, ((0, 2), (2, 64)))
    mix_weight = centred(splits[3], (C, C), C ** -0.5, 1.0)
    spec_weight = centred(splits[4], (2, M, PAIRS, C, C), 0.5, 3.0, ((2, 64),), jnp.float32)
    return {"features": features, "pre_act": pre_act, "cotangent": cotangent, "mix_weight": mix_weight, "spec_weight": spec_weight}


def contract(form, left, right):
    return jnp.einsum(form, left, right, precision=lax.Precision.HIGHEST)

def twiddle(positions, freqs, length):
    products = jnp.mod(positions[:, None] * freqs[None, :], length)
    angles = products.astype(jnp.float32) * (2.0 * math.pi / length)
    return (jnp.cos(angles), jnp.sin(angles))

def gelu_slope(pre_act):
    values = pre_act.astype(jnp.float32)
    return 0.5 * (1.0 + lax.erf(values * 0.7071067811865476)) + values * jnp.exp(-0.5 * values * values) * 0.3989422804014327

def reference(features, pre_act, cotangent, mix_weight, spec_weight):
    norm_factor = 1.0 / math.sqrt(NX * G * G)
    centered = jnp.arange(M, dtype=jnp.int32) - M // 2
    cos_z, sin_z = twiddle(jnp.arange(G, dtype=jnp.int32), jnp.arange(M, dtype=jnp.int32), G)
    cos_zb = cos_z.astype(jnp.bfloat16)
    sin_zb = sin_z.astype(jnp.bfloat16)
    cos_y, sin_y = twiddle(jnp.arange(G, dtype=jnp.int32), centered, G)
    cos_x, sin_x = twiddle(jnp.arange(NX, dtype=jnp.int32), centered, NX)
    pair_index = jnp.arange(PAIRS, dtype=jnp.int32)
    hermit = jnp.where(pair_index % M == 0, 1.0, 2.0).astype(jnp.float32)
    upstream = (cotangent.astype(jnp.float32) * gelu_slope(pre_act)).astype(jnp.bfloat16)

    def spectrum(signal):
        flat = signal.reshape(-1, G)
        z_real = jnp.dot(flat, cos_zb, preferred_element_type=jnp.float32).reshape(C, NX, G, M)
        z_imag = -jnp.dot(flat, sin_zb, preferred_element_type=jnp.float32).reshape(C, NX, G, M)
        y_real = contract('cxyk,yb->cxbk', z_real, cos_y) + contract('cxyk,yb->cxbk', z_imag, sin_y)
        y_imag = contract('cxyk,yb->cxbk', z_imag, cos_y) - contract('cxyk,yb->cxbk', z_real, sin_y)
        x_real = contract('cxbk,xa->cabk', y_real, cos_x) + contract('cxbk,xa->cabk', y_imag, sin_x)
        x_imag = contract('cxbk,xa->cabk', y_imag, cos_x) - contract('cxbk,xa->cabk', y_real, sin_x)
        return (x_real.reshape(C, M, PAIRS) * norm_factor, x_imag.reshape(C, M, PAIRS) * norm_factor)

    def per_sample(inputs_pair):
        u_real, u_imag = spectrum(inputs_pair[0])
        h_real, h_imag = spectrum(inputs_pair[1])
        return (u_real, u_imag, h_real * hermit, h_imag * hermit)
    u_real, u_imag, h_real, h_imag = lax.map(per_sample, (features, upstream))
    weight_real = spec_weight[0]
    weight_imag = spec_weight[1]
    grad_real = contract('soap,siap->apoi', h_real, u_real) + contract('soap,siap->apoi', h_imag, u_imag)
    grad_imag = contract('soap,siap->apoi', h_imag, u_real) - contract('soap,siap->apoi', h_real, u_imag)

    def backward(inputs_pair):
        hr_one, hi_one, up_one = inputs_pair
        d_real = contract('apoi,oap->iap', weight_real, hr_one) + contract('apoi,oap->iap', weight_imag, hi_one)
        d_imag = contract('apoi,oap->iap', weight_real, hi_one) - contract('apoi,oap->iap', weight_imag, hr_one)
        d_real = d_real.reshape(C, M, M, M)
        d_imag = d_imag.reshape(C, M, M, M)
        x_real = contract('iabk,xa->ixbk', d_real, cos_x) - contract('iabk,xa->ixbk', d_imag, sin_x)
        x_imag = contract('iabk,xa->ixbk', d_real, sin_x) + contract('iabk,xa->ixbk', d_imag, cos_x)
        y_real = contract('ixbk,yb->ixyk', x_real, cos_y) - contract('ixbk,yb->ixyk', x_imag, sin_y)
        y_imag = contract('ixbk,yb->ixyk', x_real, sin_y) + contract('ixbk,yb->ixyk', x_imag, cos_y)
        spatial = (contract('ixyk,zk->ixyz', y_real, cos_z) - contract('ixyk,zk->ixyz', y_imag, sin_z)) * norm_factor
        mixing = jnp.dot(mix_weight.T, up_one.reshape(C, -1), preferred_element_type=jnp.float32).reshape(C, NX, G, G)
        return (mixing + spatial).astype(jnp.bfloat16)
    grad_field = lax.map(backward, (h_real, h_imag, upstream))
    return (grad_field, jnp.stack([grad_real, grad_imag]))
```

```python
import functools
import math

import jax
import jax.numpy as jnp
import ml_dtypes
import numpy as np
from jax import lax
from jax.experimental import pallas as pl
from jax.experimental.pallas import tpu as pltpu
from jax.sharding import PartitionSpec as P

MESH = pl.DeviceIdType.MESH
BF = jnp.bfloat16
F32 = jnp.float32
C = 32
M = 32
G = 128
NX = 128
NDEV = 128
NRM = 1.0 / math.sqrt(NX * G * G)


def split_np(values):
    high = values.astype(ml_dtypes.bfloat16)
    low = (values - high.astype(np.float64)).astype(ml_dtypes.bfloat16)
    return high, low


def tables():
    freq = np.arange(M) - M // 2
    pos = np.arange(G)

    def waves(positions, freqs):
        angles = np.mod(positions[:, None] * freqs[None, :], G) * (2.0 * math.pi / G)
        return np.cos(angles), np.sin(angles)

    cos_z, sin_z = waves(pos, np.arange(M))
    cos_c, sin_c = waves(pos, freq)
    cz = cos_z.reshape(G, 4, 8)
    sz = sin_z.reshape(G, 4, 8)
    wz = np.zeros((2, G, 2, 4, 2, 2, 8))
    for x in range(2):
        wz[x, :, 0, :, x, 0] = cz
        wz[x, :, 0, :, x, 1] = -sz
        wz[x, :, 1, :, x, 0] = -sz
        wz[x, :, 1, :, x, 1] = -cz
    wz = wz.reshape(256, 256).astype(ml_dtypes.bfloat16)
    ty = np.concatenate([cos_c.T, sin_c.T], axis=1)
    ty = np.concatenate(split_np(ty), axis=0)
    tx = np.zeros((2, M, NX, 2))
    tx[0, :, :, 0] = cos_c.T
    tx[0, :, :, 1] = sin_c.T
    tx[1, :, :, 0] = -sin_c.T
    tx[1, :, :, 1] = cos_c.T
    tx = tx.reshape(64, 256)
    txh = np.concatenate(split_np(tx * NRM), axis=0)
    xh, xl = split_np(tx.T.copy())
    xs = np.concatenate([xh, xh, xl], axis=1)
    ys = np.zeros((2, G, 2, M))
    ys[0, :, 0] = cos_c
    ys[0, :, 1] = -sin_c
    ys[1, :, 0] = sin_c
    ys[1, :, 1] = cos_c
    yh, yl = split_np(ys.reshape(256, 64) * NRM)
    ys = np.concatenate([yh, yh, yl], axis=1)
    zs = np.zeros((2, 4, 8, 4, 4, G))
    ck = cos_z.T.reshape(8, 4, G).transpose(1, 0, 2)
    sk = sin_z.T.reshape(8, 4, G).transpose(1, 0, 2)
    for i in range(4):
        zs[0, :, :, i, i] = ck
        zs[1, :, :, i, i] = -sk
    zh, zl = split_np(zs.reshape(256, 512))
    eye8 = np.eye(8)
    spread = np.broadcast_to(eye8[None, :, :, None], (C, 8, 8, C)).reshape(256, 256)
    order = np.einsum("cd,kl->ckld", np.eye(C), eye8).reshape(256, 256)
    rep = np.repeat(np.eye(C), 16, axis=0)
    names = dict(wz=wz, ty=ty, tx=txh, xs=xs, ys=ys, zh=zh, zl=zl, spread=spread, order=order, rep=rep)
    return {name: np.ascontiguousarray(v).astype(ml_dtypes.bfloat16) for name, v in names.items()}


def halves(values):
    high = values.astype(BF)
    return high, (values - high.astype(F32)).astype(BF)


def dot(left, right):
    return jnp.dot(left, right, preferred_element_type=F32)


def gelu_slope(values):
    return 0.5 * (1.0 + lax.erf(values * 0.7071067811865476)) + values * (
        jnp.exp(-0.5 * values * values) * 0.3989422804014327
    )


def exchange_lanes(tiles, unit, lane):
    tiles = list(tiles)
    step = 1
    while step < len(tiles):
        keep = (lane // (unit * step)) % 2 == 0
        for i in range(len(tiles)):
            if i & step:
                continue
            low, high = tiles[i], tiles[i | step]
            tiles[i] = jnp.where(keep, low, pltpu.roll(high, unit * step, 1))
            tiles[i | step] = jnp.where(keep, pltpu.roll(low, 128 - unit * step, 1), high)
        step *= 2
    return tiles


def kernel(
    feat_hbm, pre_hbm, cot_hbm, mix_ref, spec_hbm,
    wz, ty, tx, xs, ys, zh, zl, spread, order, rep,
    field_hbm, grad_hbm,
    feat, pre, cot, wraw, up, wpack, ysc, sh, su, rh, ru, sr, rr, hx, gpack, gout, mixed, kron, fout,
    in_sems, h_sems, u_sems, r_sems, out_sems,
):
    space = lax.axis_index("space")
    samp = lax.axis_index("samp")
    me = space * 2 + samp
    slot = samp * 64 + space
    quarter = lax.rem(me, 4)

    copy_pre = pltpu.make_async_copy(pre_hbm, pre, in_sems.at[0])
    copy_cot = pltpu.make_async_copy(cot_hbm, cot, in_sems.at[1])
    copy_feat = pltpu.make_async_copy(feat_hbm, feat, in_sems.at[2])
    copy_spec = pltpu.make_async_copy(
        spec_hbm.at[:, pl.ds(samp * 256, 256), :], wraw, in_sems.at[3]
    )
    copy_pre.start()
    copy_cot.start()
    copy_feat.start()
    copy_spec.start()

    def device(d):
        return (lax.div(d, 2), lax.rem(d, 2))

    barrier = pltpu.get_barrier_semaphore()

    def greet(j, carry):
        d = lax.rem(me + j, NDEV)
        pl.semaphore_signal(barrier, inc=1, device_id=device(d), device_id_type=MESH)
        return carry

    lax.fori_loop(1, NDEV, greet, 0)

    lane8 = lax.broadcasted_iota(jnp.int32, (8, 128), 1)

    def spectra(source, half, out):
        def pair(cp, carry):
            c0 = half * 16 + cp * 2
            z0 = dot(jnp.concatenate([source[c0, 0], source[c0, 1]], axis=1), wz[...])
            z1 = dot(jnp.concatenate([source[c0 + 1, 0], source[c0 + 1, 1]], axis=1), wz[...])
            r = jnp.concatenate(
                [
                    jnp.concatenate([z0[:, :128], z1[:, :128]], axis=1),
                    jnp.concatenate([z0[:, 128:], z1[:, 128:]], axis=1),
                ],
                axis=0,
            )
            high, low = halves(r)
            p = dot(ty[...], high)
            y = p[:32] + p[32:] + dot(ty[0:32, :], low)
            ysc[cp * 2] = y[:, :128]
            ysc[cp * 2 + 1] = y[:, 128:]
            return carry

        lax.fori_loop(0, 8, pair, 0)
        for bo in range(4):
            tiles = [ysc[c, bo * 8 : bo * 8 + 8, :] for c in range(16)]
            tiles = exchange_lanes(tiles, 8, lane8)
            for n in range(16):
                q, xr = n // 4, n % 4
                out[pl.ds(bo * 256 + q * 8 + xr * 2 + half, 8, stride=32), :] = tiles[n]

    def send_all(src, src_at, dst, dst_at, sems, keep_sem):
        def send(j, carry):
            d = lax.rem(me + j, NDEV)
            pltpu.make_async_remote_copy(
                src_ref=src.at[pl.ds(pl.multiple_of(src_at(d) * 8, 8), 8), :],
                dst_ref=dst.at[pl.ds(pl.multiple_of(dst_at * 8, 8), 8), :],
                send_sem=sems.at[0],
                recv_sem=sems.at[1],
                device_id=device(d),
                device_id_type=MESH,
            ).start()
            return carry

        lax.fori_loop(1, NDEV, send, 0)
        own = pltpu.make_async_copy(
            src.at[pl.ds(pl.multiple_of(src_at(me) * 8, 8), 8), :],
            dst.at[pl.ds(pl.multiple_of(dst_at * 8, 8), 8), :],
            keep_sem,
        )
        own.start()
        return own

    def arrived(ref, sem):
        part = ref.at[pl.ds(0, (NDEV - 1) * 8), :]
        pltpu.make_async_copy(part, part, sem).wait()

    copy_pre.wait()
    copy_cot.wait()

    def slope(c, carry):
        for x in range(2):
            values = cot[c, x].astype(F32) * gelu_slope(pre[c, x].astype(F32))
            up[c, x] = values.astype(BF)
        return carry

    lax.fori_loop(0, C, slope, 0)
    for half in range(2):
        spectra(up, half, sh)
    pl.semaphore_wait(barrier, NDEV - 1)
    own_h = send_all(sh, lambda d: d, rh, slot, h_sems, h_sems.at[2])

    copy_feat.wait()
    for half in range(2):
        spectra(feat, half, su)
    own_u = send_all(su, lambda d: d, ru, slot, u_sems, u_sems.at[2])

    copy_spec.wait()

    def pack(a, carry):
        for ri in range(2):
            for j in range(2):
                parts = [
                    wraw[ri * 32 + a, pl.ds((j * 4 + k) * 32, 32), :] for k in range(4)
                ]
                wpack[ri * 2 + j, pl.ds(a, 32, stride=32), :] = jnp.concatenate(parts, axis=1)
        return carry

    lax.fori_loop(0, M, pack, 0)

    turned = lax.dot_general(
        rep[...], mix_ref[...], (((1,), (1,)), ((), ())), preferred_element_type=F32
    ).astype(BF)
    wide = lax.dot_general(
        turned, rep[...], (((1,), (1,)), ((), ())), preferred_element_type=F32
    )
    row = lax.broadcasted_iota(jnp.int32, (512, 512), 0)
    col = lax.broadcasted_iota(jnp.int32, (512, 512), 1)
    kron[...] = jnp.where(lax.rem(row, 16) == lax.rem(col, 16), wide, 0.0).astype(BF)

    def mixing(yb, carry):
        y0 = pl.multiple_of(yb * 16, 16)
        for x in range(2):
            block = up[:, x, pl.ds(y0, 16), :].reshape(512, 128)
            mixed[:, x, pl.ds(y0, 16), :] = dot(kron[...], block).reshape(C, 16, 128)
        return carry

    lax.fori_loop(0, 8, mixing, 0)

    def x_sums(ref, t):
        r = jnp.concatenate(
            [ref[pl.ds(t * 512, 256, stride=2), :], ref[pl.ds(t * 512 + 1, 256, stride=2), :]],
            axis=1,
        )
        high, low = halves(r)
        p = dot(tx[...], high)
        return p[:64] + p[64:] + dot(tx[0:64, :], low)

    arrived(rh, h_sems.at[1])
    own_h.wait()
    lane256 = lax.broadcasted_iota(jnp.int32, (1, 256), 1)
    single = jnp.logical_and(lax.rem(lane256, 8) == 0, quarter == 0)
    hermit = jnp.where(single, 1.0, 2.0).astype(F32)
    h = jnp.concatenate([x_sums(rh, 0), x_sums(rh, 1)], axis=0) * hermit
    h_high, h_low = halves(h)
    h_both = jnp.concatenate([h_high, h_low], axis=0)

    def spread_one(o, carry):
        picked = jnp.where(lax.div(lane256, 8) == o, h_both, jnp.zeros_like(h_both))
        p = dot(picked, spread[...])
        hx[o] = p[:128] + p[128:]
        return carry

    lax.fori_loop(0, C, spread_one, 0)

    for t in range(2):
        parts = []
        for j in range(2):
            lanes = slice(j * 128, j * 128 + 128)

            def mode_sum(o, carry):
                d_real, d_imag = carry
                h_real = hx[o, t * 64 : t * 64 + 32, lanes]
                h_imag = hx[o, t * 64 + 32 : t * 64 + 64, lanes]
                rows = pl.ds(pl.multiple_of(o * 32, 32), 32)
                w_real = wpack[j, rows, :]
                w_imag = wpack[2 + j, rows, :]
                return (
                    d_real + w_real * h_real + w_imag * h_imag,
                    d_imag + w_real * h_imag - w_imag * h_real,
                )

            zero = jnp.zeros((32, 128), F32)
            d_real, d_imag = lax.fori_loop(0, C, mode_sum, (zero, zero))
            parts.append(jnp.concatenate([d_real, d_imag], axis=0))
        high, low = halves(jnp.concatenate(parts, axis=1))
        x_syn = dot(xs[...], jnp.concatenate([high, low, high], axis=0))
        sr[pl.ds(t * 512, 256, stride=2), :] = x_syn[:, :128]
        sr[pl.ds(t * 512 + 1, 256, stride=2), :] = x_syn[:, 128:]
    own_r = send_all(sr, lambda d: lax.rem(d, 2) * 64 + lax.div(d, 2), rr, me, r_sems, r_sems.at[2])

    arrived(ru, u_sems.at[1])
    own_u.wait()
    u = jnp.concatenate([x_sums(ru, 0), x_sums(ru, 1)], axis=0)
    u_high, u_low = halves(u)
    p = dot(jnp.concatenate([u_high, u_low], axis=0), order[...])
    u = p[:128] + p[128:]

    for j in range(2):
        lanes = slice(j * 128, j * 128 + 128)
        for ah in range(2):
            u_parts = [u[r * 32 + ah * 16 : r * 32 + ah * 16 + 16, lanes] for r in range(4)]

            def outer(o, carry):
                hs = [hx[o, r * 32 + ah * 16 : r * 32 + ah * 16 + 16, lanes] for r in range(4)]
                real = hs[0] * u_parts[0] + hs[1] * u_parts[1] + hs[2] * u_parts[2] + hs[3] * u_parts[3]
                imag = hs[1] * u_parts[0] - hs[0] * u_parts[1] + hs[3] * u_parts[2] - hs[2] * u_parts[3]
                rows = pl.ds(pl.multiple_of(o * 32 + ah * 16, 16), 16)
                gpack[j, rows, :] = real
                gpack[2 + j, rows, :] = imag
                return carry

            lax.fori_loop(0, C, outer, 0)

    def unpack(a, carry):
        for ri in range(2):
            for j in range(2):
                tile = gpack[ri * 2 + j, pl.ds(a, 32, stride=32), :]
                for k in range(4):
                    gout[ri * 32 + a, pl.ds((j * 4 + k) * 32, 32), :] = tile[:, k * 32 : k * 32 + 32]
        return carry

    lax.fori_loop(0, M, unpack, 0)
    copy_grad = pltpu.make_async_copy(gout, grad_hbm, out_sems.at[0])
    copy_grad.start()

    arrived(rr, r_sems.at[1])
    own_r.wait()
    for x in range(2):
        tiles = [[None] * 8 for _ in range(8)]
        for ri in range(2):
            for bo in range(4):
                loaded = [
                    rr[pl.ds(bo * 256 + (n // 2) * 8 + x * 4 + ri * 2 + n % 2, 8, stride=32), :]
                    for n in range(8)
                ]
                for ig, tile in enumerate(exchange_lanes(loaded, 4, lane8)):
                    tiles[ig][ri * 4 + bo] = tile
        for ig in range(8):
            high, low = halves(jnp.concatenate(tiles[ig], axis=0))
            y_syn = dot(ys[...], jnp.concatenate([high, low, high], axis=0))
            high, low = halves(jnp.concatenate([y_syn[:128], y_syn[128:]], axis=1))
            z_syn = dot(high, zh[...]) + dot(low, zh[...]) + dot(high, zl[...])
            for i in range(4):
                total = mixed[ig * 4 + i, x] + z_syn[:, i * 128 : i * 128 + 128]
                fout[ig * 4 + i, x] = total.astype(BF)
    copy_field = pltpu.make_async_copy(fout, field_hbm, out_sems.at[1])
    copy_field.start()
    arrived(sh, h_sems.at[0])
    arrived(su, u_sems.at[0])
    arrived(sr, r_sems.at[0])
    copy_field.wait()
    copy_grad.wait()


def shards(features, pre_act, cotangent, mix_weight, spec_weight):
    planes = (C, 2, G, G)
    consts = tables()
    names = ("wz", "ty", "tx", "xs", "ys", "zh", "zl", "spread", "order", "rep")
    anywhere = pl.BlockSpec(memory_space=pl.ANY)
    inside = pl.BlockSpec(memory_space=pltpu.VMEM)
    message = pltpu.VMEM((NDEV * 8, 128), F32)
    field, grad = pl.pallas_call(
        kernel,
        out_shape=(
            jax.ShapeDtypeStruct(planes, BF),
            jax.ShapeDtypeStruct((64, 256, 32), F32),
        ),
        in_specs=[anywhere] * 3 + [inside] + [anywhere] + [inside] * len(names),
        out_specs=(anywhere, anywhere),
        scratch_shapes=[
            pltpu.VMEM(planes, BF),
            pltpu.VMEM(planes, BF),
            pltpu.VMEM(planes, BF),
            pltpu.VMEM((64, 256, 32), F32),
            pltpu.VMEM(planes, BF),
            pltpu.VMEM((4, 1024, 128), F32),
            pltpu.VMEM((16, 32, 128), F32),
            message, message, message, message, message, message,
            pltpu.VMEM((C, 128, 256), F32),
            pltpu.VMEM((4, 1024, 128), F32),
            pltpu.VMEM((64, 256, 32), F32),
            pltpu.VMEM(planes, F32),
            pltpu.VMEM((512, 512), BF),
            pltpu.VMEM(planes, BF),
            pltpu.SemaphoreType.DMA((4,)),
            pltpu.SemaphoreType.DMA((3,)),
            pltpu.SemaphoreType.DMA((3,)),
            pltpu.SemaphoreType.DMA((3,)),
            pltpu.SemaphoreType.DMA((2,)),
        ],
        compiler_params=pltpu.CompilerParams(
            collective_id=0, has_side_effects=True, vmem_limit_bytes=62 * 2**20
        ),
    )(
        features.reshape(planes),
        pre_act.reshape(planes),
        cotangent.reshape(planes),
        mix_weight,
        spec_weight.reshape(64, 512, 32),
        *[jnp.asarray(consts[name]) for name in names],
    )
    return field.reshape(features.shape), grad.reshape(2, M, 8, C, C)


def solution(mesh):
    placed = P("samp", None, "space", None, None)
    return jax.shard_map(
        shards,
        mesh=mesh,
        in_specs=(placed, placed, placed, P(), P(None, None, "space", None, None)),
        out_specs=(placed, P(None, None, ("space", "samp"), None, None)),
        check_vma=False,
    )
```

```python
import math

import jax
import jax.numpy as jnp
import ml_dtypes
import numpy as np
from jax import lax
from jax.experimental import pallas as pl
from jax.experimental.pallas import tpu as pltpu
from jax.sharding import PartitionSpec as P

MESH = pl.DeviceIdType.MESH
BF = jnp.bfloat16
F32 = jnp.float32
C = 32
M = 32
G = 128
NX = 128
NDEV = 128
NRM = 1.0 / math.sqrt(NX * G * G)


def split_np(values):
    high = values.astype(ml_dtypes.bfloat16)
    low = (values - high.astype(np.float64)).astype(ml_dtypes.bfloat16)
    return high, low


def tables():
    freq = np.arange(M) - M // 2
    pos = np.arange(G)

    def waves(positions, freqs):
        angles = np.mod(positions[:, None] * freqs[None, :], G) * (2.0 * math.pi / G)
        return np.cos(angles), np.sin(angles)

    cos_z, sin_z = waves(pos, np.arange(M))
    cos_c, sin_c = waves(pos, freq)
    cz = cos_z.reshape(G, 4, 8)
    sz = sin_z.reshape(G, 4, 8)
    wz = np.zeros((2, G, 2, 4, 2, 2, 8))
    for x in range(2):
        wz[x, :, 0, :, x, 0] = cz
        wz[x, :, 0, :, x, 1] = -sz
        wz[x, :, 1, :, x, 0] = -sz
        wz[x, :, 1, :, x, 1] = -cz
    wz = wz.reshape(256, 256).astype(ml_dtypes.bfloat16)
    ty = np.concatenate([cos_c.T, sin_c.T], axis=1)
    ty = np.concatenate(split_np(ty), axis=0)
    tx = np.zeros((2, M, NX, 2))
    tx[0, :, :, 0] = cos_c.T
    tx[0, :, :, 1] = sin_c.T
    tx[1, :, :, 0] = -sin_c.T
    tx[1, :, :, 1] = cos_c.T
    tx = tx.reshape(64, 256)
    txh = np.concatenate(split_np(tx * NRM), axis=0)
    xh, xl = split_np(tx.T.copy())
    xs = np.concatenate([xh, xh, xl], axis=1)
    ys = np.zeros((2, G, 2, M))
    ys[0, :, 0] = cos_c
    ys[0, :, 1] = -sin_c
    ys[1, :, 0] = sin_c
    ys[1, :, 1] = cos_c
    yh, yl = split_np(ys.reshape(256, 64) * NRM)
    ys = np.concatenate([yh, yh, yl], axis=1)
    zs = np.zeros((2, 4, 8, 4, 4, G))
    ck = cos_z.T.reshape(8, 4, G).transpose(1, 0, 2)
    sk = sin_z.T.reshape(8, 4, G).transpose(1, 0, 2)
    for i in range(4):
        zs[0, :, :, i, i] = ck
        zs[1, :, :, i, i] = -sk
    zh, zl = split_np(zs.reshape(256, 512))
    eye8 = np.eye(8)
    spread = np.broadcast_to(eye8[None, :, :, None], (C, 8, 8, C)).reshape(256, 256)
    order = np.einsum("cd,kl->ckld", np.eye(C), eye8).reshape(256, 256)
    rep = np.repeat(np.eye(C), 16, axis=0)
    names = dict(wz=wz, ty=ty, tx=txh, xs=xs, ys=ys, zh=zh, zl=zl, spread=spread, order=order, rep=rep)
    return {name: np.ascontiguousarray(v).astype(ml_dtypes.bfloat16) for name, v in names.items()}


def halves(values):
    high = values.astype(BF)
    return high, (values - high.astype(F32)).astype(BF)


def dot(left, right):
    return jnp.dot(left, right, preferred_element_type=F32)


def gelu_slope(values):
    return 0.5 * (1.0 + lax.erf(values * 0.7071067811865476)) + values * (
        jnp.exp(-0.5 * values * values) * 0.3989422804014327
    )


def exchange_lanes(tiles, unit, lane):
    tiles = list(tiles)
    step = 1
    while step < len(tiles):
        keep = (lane // (unit * step)) % 2 == 0
        for i in range(len(tiles)):
            if i & step:
                continue
            low, high = tiles[i], tiles[i | step]
            tiles[i] = jnp.where(keep, low, pltpu.roll(high, unit * step, 1))
            tiles[i | step] = jnp.where(keep, pltpu.roll(low, 128 - unit * step, 1), high)
        step *= 2
    return tiles


def gather(
    feat_hbm, pre_hbm, cot_hbm, mix_ref, spec_hbm,
    wz, ty, tx, xs, spread, order, rep,
    rr, mixed, gout,
    feat, pre, cot, wraw, up, wpack, ysc, sh, su, rh, ru, sr, hx, gpack, kron,
    in_sems, h_sems, u_sems, r_sems,
):
    space = lax.axis_index("space")
    samp = lax.axis_index("samp")
    me = space * 2 + samp
    slot = samp * 64 + space
    quarter = lax.rem(me, 4)

    def parts_of(hbm, vmem, first):
        rows = [pl.ds(part * 8, 8) for part in range(4)]
        return [
            pltpu.make_async_copy(hbm.at[r], vmem.at[r], in_sems.at[first + part])
            for part, r in enumerate(rows)
        ]

    copies_pre = parts_of(pre_hbm, pre, 0)
    copies_cot = parts_of(cot_hbm, cot, 4)
    copies_feat = parts_of(feat_hbm, feat, 8)
    copy_spec = pltpu.make_async_copy(
        spec_hbm.at[:, pl.ds(samp * 256, 256), :], wraw, in_sems.at[12]
    )
    for part in range(4):
        copies_pre[part].start()
        copies_cot[part].start()
    for part in range(4):
        copies_feat[part].start()
    copy_spec.start()

    def device(d):
        return (lax.div(d, 2), lax.rem(d, 2))

    barrier = pltpu.get_barrier_semaphore()

    def greet(j):
        d = lax.rem(me + j, NDEV)
        pl.semaphore_signal(barrier, inc=1, device_id=device(d), device_id_type=MESH)

    lane8 = lax.broadcasted_iota(jnp.int32, (8, 128), 1)

    def spectra(source, half, out, before):
        for cp in range(8):
            c0 = half * 16 + cp * 2
            before(c0)
            z0 = dot(jnp.concatenate([source[c0, 0], source[c0, 1]], axis=1), wz[...])
            z1 = dot(jnp.concatenate([source[c0 + 1, 0], source[c0 + 1, 1]], axis=1), wz[...])
            r = jnp.concatenate(
                [
                    jnp.concatenate([z0[:, :128], z1[:, :128]], axis=1),
                    jnp.concatenate([z0[:, 128:], z1[:, 128:]], axis=1),
                ],
                axis=0,
            )
            high, low = halves(r)
            p = dot(ty[...], high)
            y = p[:32] + p[32:] + dot(ty[0:32, :], low)
            ysc[cp * 2] = y[:, :128]
            ysc[cp * 2 + 1] = y[:, 128:]
        for bo in range(4):
            tiles = [ysc[c, bo * 8 : bo * 8 + 8, :] for c in range(16)]
            tiles = exchange_lanes(tiles, 8, lane8)
            for n in range(16):
                q, xr = n // 4, n % 4
                out[pl.ds(bo * 256 + q * 8 + xr * 2 + half, 8, stride=32), :] = tiles[n]

    def send_all(src, src_at, dst, dst_at, sems, keep_sem):
        def send(j, carry):
            d = lax.rem(me + j, NDEV)
            pltpu.make_async_remote_copy(
                src_ref=src.at[pl.ds(pl.multiple_of(src_at(d) * 8, 8), 8), :],
                dst_ref=dst.at[pl.ds(pl.multiple_of(dst_at * 8, 8), 8), :],
                send_sem=sems.at[0],
                recv_sem=sems.at[1],
                device_id=device(d),
                device_id_type=MESH,
            ).start()
            return carry

        lax.fori_loop(1, NDEV, send, 0)
        own = pltpu.make_async_copy(
            src.at[pl.ds(pl.multiple_of(src_at(me) * 8, 8), 8), :],
            dst.at[pl.ds(pl.multiple_of(dst_at * 8, 8), 8), :],
            keep_sem,
        )
        own.start()
        return own

    def arrived(ref, sem):
        part = ref.at[pl.ds(0, (NDEV - 1) * 8), :]
        pltpu.make_async_copy(part, part, sem).wait()

    def slope(c0):
        if c0 % 8 == 0:
            copies_pre[c0 // 8].wait()
            copies_cot[c0 // 8].wait()
        for c in (c0, c0 + 1):
            for x in range(2):
                values = cot[c, x].astype(F32) * gelu_slope(pre[c, x].astype(F32))
                up[c, x] = values.astype(BF)
        for j in range(c0 * 4, c0 * 4 + 8):
            if j:
                greet(j)

    for half in range(2):
        spectra(up, half, sh, slope)
    pl.semaphore_wait(barrier, NDEV - 1)
    own_h = send_all(sh, lambda d: d, rh, slot, h_sems, h_sems.at[2])

    def loaded_feat(c0):
        if c0 % 8 == 0:
            copies_feat[c0 // 8].wait()

    for half in range(2):
        spectra(feat, half, su, loaded_feat)
    own_u = send_all(su, lambda d: d, ru, slot, u_sems, u_sems.at[2])

    copy_spec.wait()

    def pack(a, carry):
        for ri in range(2):
            for j in range(2):
                parts = [
                    wraw[ri * 32 + a, pl.ds((j * 4 + k) * 32, 32), :] for k in range(4)
                ]
                wpack[ri * 2 + j, pl.ds(a, 32, stride=32), :] = jnp.concatenate(parts, axis=1)
        return carry

    lax.fori_loop(0, M, pack, 0)

    def x_sums(ref, t):
        r = jnp.concatenate(
            [ref[pl.ds(t * 512, 256, stride=2), :], ref[pl.ds(t * 512 + 1, 256, stride=2), :]],
            axis=1,
        )
        high, low = halves(r)
        p = dot(tx[...], high)
        return p[:64] + p[64:] + dot(tx[0:64, :], low)

    arrived(rh, h_sems.at[1])
    own_h.wait()
    lane256 = lax.broadcasted_iota(jnp.int32, (1, 256), 1)
    single = jnp.logical_and(lax.rem(lane256, 8) == 0, quarter == 0)
    hermit = jnp.where(single, 1.0, 2.0).astype(F32)
    h = jnp.concatenate([x_sums(rh, 0), x_sums(rh, 1)], axis=0) * hermit
    h_high, h_low = halves(h)
    h_both = jnp.concatenate([h_high, h_low], axis=0)

    def mode_sum(o, sums):
        picked = jnp.where(lax.div(lane256, 8) == o, h_both, jnp.zeros_like(h_both))
        p = dot(picked, spread[...])
        spread_h = p[:128] + p[128:]
        hx[o] = spread_h
        rows = pl.ds(pl.multiple_of(o * 32, 32), 32)
        later = []
        for j in range(2):
            w_real = wpack[j, rows, :]
            w_imag = wpack[2 + j, rows, :]
            for t in range(2):
                h_real = spread_h[t * 64 : t * 64 + 32, j * 128 : j * 128 + 128]
                h_imag = spread_h[t * 64 + 32 : t * 64 + 64, j * 128 : j * 128 + 128]
                d_real, d_imag = sums[(j * 2 + t) * 2], sums[(j * 2 + t) * 2 + 1]
                later.append(d_real + w_real * h_real + w_imag * h_imag)
                later.append(d_imag + w_real * h_imag - w_imag * h_real)
        return tuple(later)

    zero = jnp.zeros((32, 128), F32)
    sums = lax.fori_loop(0, C, mode_sum, (zero,) * 8, unroll=4)
    for t in range(2):
        left = jnp.concatenate([sums[t * 2], sums[t * 2 + 1]], axis=0)
        right = jnp.concatenate([sums[4 + t * 2], sums[5 + t * 2]], axis=0)
        high, low = halves(jnp.concatenate([left, right], axis=1))
        x_syn = dot(xs[...], jnp.concatenate([high, low, high], axis=0))
        sr[pl.ds(t * 512, 256, stride=2), :] = x_syn[:, :128]
        sr[pl.ds(t * 512 + 1, 256, stride=2), :] = x_syn[:, 128:]
    own_r = send_all(sr, lambda d: lax.rem(d, 2) * 64 + lax.div(d, 2), rr, me, r_sems, r_sems.at[2])

    arrived(ru, u_sems.at[1])
    own_u.wait()
    u = jnp.concatenate([x_sums(ru, 0), x_sums(ru, 1)], axis=0)
    u_high, u_low = halves(u)
    p = dot(jnp.concatenate([u_high, u_low], axis=0), order[...])
    u = p[:128] + p[128:]

    for j in range(2):
        lanes = slice(j * 128, j * 128 + 128)
        for ah in range(2):
            u_parts = [u[r * 32 + ah * 16 : r * 32 + ah * 16 + 16, lanes] for r in range(4)]

            def outer(o, carry):
                hs = [hx[o, r * 32 + ah * 16 : r * 32 + ah * 16 + 16, lanes] for r in range(4)]
                real = hs[0] * u_parts[0] + hs[1] * u_parts[1] + hs[2] * u_parts[2] + hs[3] * u_parts[3]
                imag = hs[1] * u_parts[0] - hs[0] * u_parts[1] + hs[3] * u_parts[2] - hs[2] * u_parts[3]
                rows = pl.ds(pl.multiple_of(o * 32 + ah * 16, 16), 16)
                gpack[j, rows, :] = real
                gpack[2 + j, rows, :] = imag
                return carry

            lax.fori_loop(0, C, outer, 0)

    def unpack(a, carry):
        for ri in range(2):
            for j in range(2):
                tile = gpack[ri * 2 + j, pl.ds(a, 32, stride=32), :]
                for k in range(4):
                    gout[ri * 32 + a, pl.ds((j * 4 + k) * 32, 32), :] = tile[:, k * 32 : k * 32 + 32]
        return carry

    lax.fori_loop(0, M, unpack, 0)

    turned = lax.dot_general(
        rep[...], mix_ref[...], (((1,), (1,)), ((), ())), preferred_element_type=F32
    ).astype(BF)
    wide = lax.dot_general(
        turned, rep[...], (((1,), (1,)), ((), ())), preferred_element_type=F32
    )
    row = lax.broadcasted_iota(jnp.int32, (512, 512), 0)
    col = lax.broadcasted_iota(jnp.int32, (512, 512), 1)
    kron[...] = jnp.where(lax.rem(row, 16) == lax.rem(col, 16), wide, 0.0).astype(BF)

    def mixing(yb, carry):
        y0 = pl.multiple_of(yb * 16, 16)
        for x in range(2):
            block = up[:, x, pl.ds(y0, 16), :].reshape(512, 128)
            mixed[:, x, pl.ds(y0, 16), :] = dot(kron[...], block).reshape(C, 16, 128)
        return carry

    lax.fori_loop(0, 8, mixing, 0)

    arrived(rr, r_sems.at[1])
    own_r.wait()
    arrived(sh, h_sems.at[0])
    arrived(su, u_sems.at[0])
    arrived(sr, r_sems.at[0])


def synthesis(rr, mixed, gout, ys, zh, zl, field_hbm, grad_hbm, fout, sems):
    lane8 = lax.broadcasted_iota(jnp.int32, (8, 128), 1)
    copy_grad = pltpu.make_async_copy(gout, grad_hbm, sems.at[8])
    copy_grad.start()
    tiles = [[[None] * 8 for _ in range(8)] for _ in range(2)]
    for x in range(2):
        for ri in range(2):
            for bo in range(4):
                loaded = [
                    rr[pl.ds(bo * 256 + (n // 2) * 8 + x * 4 + ri * 2 + n % 2, 8, stride=32), :]
                    for n in range(8)
                ]
                for ig, tile in enumerate(exchange_lanes(loaded, 4, lane8)):
                    tiles[x][ig][ri * 4 + bo] = tile
    copies = []
    for ig in range(8):
        for x in range(2):
            high, low = halves(jnp.concatenate(tiles[x][ig], axis=0))
            y_syn = dot(ys[...], jnp.concatenate([high, low, high], axis=0))
            high, low = halves(jnp.concatenate([y_syn[:128], y_syn[128:]], axis=1))
            z_syn = dot(high, zh[...]) + dot(low, zh[...]) + dot(high, zl[...])
            for i in range(4):
                total = mixed[ig * 4 + i, x] + z_syn[:, i * 128 : i * 128 + 128]
                fout[ig * 4 + i, x] = total.astype(BF)
        rows = pl.ds(ig * 4, 4)
        copies.append(pltpu.make_async_copy(fout.at[rows], field_hbm.at[rows], sems.at[ig]))
        copies[-1].start()
    for copy in copies:
        copy.wait()
    copy_grad.wait()


def shards(features, pre_act, cotangent, mix_weight, spec_weight):
    planes = (C, 2, G, G)
    consts = tables()
    anywhere = pl.BlockSpec(memory_space=pl.ANY)
    inside = pl.BlockSpec(memory_space=pltpu.VMEM)
    message = pltpu.VMEM((NDEV * 8, 128), F32)
    grad_shape = (64, 256, 32)
    first = ("wz", "ty", "tx", "xs", "spread", "order", "rep")
    returned, mixed, grad = pl.pallas_call(
        gather,
        out_shape=(
            pltpu.VMEM((NDEV * 8, 128), F32),
            pltpu.VMEM(planes, F32),
            pltpu.VMEM(grad_shape, F32),
        ),
        in_specs=[anywhere] * 3 + [inside] + [anywhere] + [inside] * len(first),
        out_specs=(inside, inside, inside),
        scratch_shapes=[
            pltpu.VMEM(planes, BF),
            pltpu.VMEM(planes, BF),
            pltpu.VMEM(planes, BF),
            pltpu.VMEM(grad_shape, F32),
            pltpu.VMEM(planes, BF),
            pltpu.VMEM((4, 1024, 128), F32),
            pltpu.VMEM((16, 32, 128), F32),
            message, message, message, message, message,
            pltpu.VMEM((C, 128, 256), F32),
            pltpu.VMEM((4, 1024, 128), F32),
            pltpu.VMEM((512, 512), BF),
            pltpu.SemaphoreType.DMA((13,)),
            pltpu.SemaphoreType.DMA((3,)),
            pltpu.SemaphoreType.DMA((3,)),
            pltpu.SemaphoreType.DMA((3,)),
        ],
        compiler_params=pltpu.CompilerParams(
            collective_id=0, has_side_effects=True, vmem_limit_bytes=44 * 2**20
        ),
    )(
        features.reshape(planes),
        pre_act.reshape(planes),
        cotangent.reshape(planes),
        mix_weight,
        spec_weight.reshape(64, 512, 32),
        *[jnp.asarray(consts[name]) for name in first],
    )
    second = ("ys", "zh", "zl")
    field, grad = pl.pallas_call(
        synthesis,
        out_shape=(
            jax.ShapeDtypeStruct(planes, BF),
            jax.ShapeDtypeStruct(grad_shape, F32),
        ),
        in_specs=[inside] * (3 + len(second)),
        out_specs=(anywhere, anywhere),
        scratch_shapes=[
            pltpu.VMEM(planes, BF),
            pltpu.SemaphoreType.DMA((9,)),
        ],
        compiler_params=pltpu.CompilerParams(vmem_limit_bytes=40 * 2**20),
    )(returned, mixed, grad, *[jnp.asarray(consts[name]) for name in second])
    return field.reshape(features.shape), grad.reshape(2, M, 8, C, C)


def solution(mesh):
    placed = P("samp", None, "space", None, None)
    return jax.shard_map(
        shards,
        mesh=mesh,
        in_specs=(placed, placed, placed, P(), P(None, None, "space", None, None)),
        out_specs=(placed, P(None, None, ("space", "samp"), None, None)),
        check_vma=False,
    )
```

```python
import math

import jax
import jax.numpy as jnp
import ml_dtypes
import numpy as np
from jax import lax
from jax.experimental import pallas as pl
from jax.experimental.pallas import tpu as pltpu
from jax.sharding import PartitionSpec as P

MESH = pl.DeviceIdType.MESH
BF = jnp.bfloat16
F32 = jnp.float32
C = 32
M = 32
G = 128
NX = 128
NDEV = 128
NRM = 1.0 / math.sqrt(NX * G * G)


def split_np(values):
    high = values.astype(ml_dtypes.bfloat16)
    low = (values - high.astype(np.float64)).astype(ml_dtypes.bfloat16)
    return high, low


def tables():
    freq = np.arange(M) - M // 2
    pos = np.arange(G)

    def waves(positions, freqs):
        angles = np.mod(positions[:, None] * freqs[None, :], G) * (2.0 * math.pi / G)
        return np.cos(angles), np.sin(angles)

    cos_z, sin_z = waves(pos, np.arange(M))
    cos_c, sin_c = waves(pos, freq)
    cz = cos_z.reshape(G, 4, 8)
    sz = sin_z.reshape(G, 4, 8)
    wz = np.zeros((2, G, 2, 4, 2, 2, 8))
    for x in range(2):
        wz[x, :, 0, :, x, 0] = cz
        wz[x, :, 0, :, x, 1] = -sz
        wz[x, :, 1, :, x, 0] = -sz
        wz[x, :, 1, :, x, 1] = -cz
    wz = wz.reshape(256, 256).astype(ml_dtypes.bfloat16)
    ty = np.concatenate([cos_c.T, sin_c.T], axis=1)
    ty = np.concatenate(split_np(ty), axis=0)
    tx = np.zeros((2, M, NX, 2))
    tx[0, :, :, 0] = cos_c.T
    tx[0, :, :, 1] = sin_c.T
    tx[1, :, :, 0] = -sin_c.T
    tx[1, :, :, 1] = cos_c.T
    tx = tx.reshape(64, 256)
    txh = np.concatenate(split_np(tx * NRM), axis=0)
    xh, xl = split_np(tx.T.copy())
    xs = np.concatenate([xh, xh, xl], axis=1)
    ys = np.zeros((2, G, 2, M))
    ys[0, :, 0] = cos_c
    ys[0, :, 1] = -sin_c
    ys[1, :, 0] = sin_c
    ys[1, :, 1] = cos_c
    yh, yl = split_np(ys.reshape(256, 64) * NRM)
    ys = np.concatenate([yh, yh, yl], axis=1)
    zs = np.zeros((2, 4, 8, 4, 4, G))
    ck = cos_z.T.reshape(8, 4, G).transpose(1, 0, 2)
    sk = sin_z.T.reshape(8, 4, G).transpose(1, 0, 2)
    for i in range(4):
        zs[0, :, :, i, i] = ck
        zs[1, :, :, i, i] = -sk
    zh, zl = split_np(zs.reshape(256, 512))
    eye8 = np.eye(8)
    spread = np.broadcast_to(eye8[None, :, :, None], (C, 8, 8, C)).reshape(256, 256)
    order = np.einsum("cd,kl->ckld", np.eye(C), eye8).reshape(256, 256)
    rep = np.repeat(np.eye(C), 16, axis=0)
    names = dict(wz=wz, ty=ty, tx=txh, xs=xs, ys=ys, zh=zh, zl=zl, spread=spread, order=order, rep=rep)
    return {name: np.ascontiguousarray(v).astype(ml_dtypes.bfloat16) for name, v in names.items()}


def halves(values):
    high = values.astype(BF)
    return high, (values - high.astype(F32)).astype(BF)


def dot(left, right):
    return jnp.dot(left, right, preferred_element_type=F32)


def gelu_slope(values):
    return 0.5 * (1.0 + lax.erf(values * 0.7071067811865476)) + values * (
        jnp.exp(-0.5 * values * values) * 0.3989422804014327
    )


def exchange_lanes(tiles, unit, lane):
    tiles = list(tiles)
    step = 1
    while step < len(tiles):
        keep = (lane // (unit * step)) % 2 == 0
        for i in range(len(tiles)):
            if i & step:
                continue
            low, high = tiles[i], tiles[i | step]
            tiles[i] = jnp.where(keep, low, pltpu.roll(high, unit * step, 1))
            tiles[i | step] = jnp.where(keep, pltpu.roll(low, 128 - unit * step, 1), high)
        step *= 2
    return tiles


def gather(
    feat_hbm, pre_hbm, cot_hbm, mix_ref, spec_hbm,
    wz, ty, tx, xs, spread, order, rep,
    rr, mixed, gout,
    feat, pre, cot, wraw, up, wpack, ysc, sh, su, rh, ru, sr, hx, gpack, kron,
    in_sems, h_sems, u_sems, r_sems, relay,
):
    space = lax.axis_index("space")
    samp = lax.axis_index("samp")
    me = space * 2 + samp
    slot = samp * 64 + space
    quarter = lax.rem(me, 4)

    def parts_of(hbm, vmem, first):
        rows = [pl.ds(part * 8, 8) for part in range(4)]
        return [
            pltpu.make_async_copy(hbm.at[r], vmem.at[r], in_sems.at[first + part])
            for part, r in enumerate(rows)
        ]

    copies_pre = parts_of(pre_hbm, pre, 0)
    copies_cot = parts_of(cot_hbm, cot, 4)
    copies_feat = parts_of(feat_hbm, feat, 8)
    copy_spec = pltpu.make_async_copy(
        spec_hbm.at[:, pl.ds(samp * 256, 256), :], wraw, in_sems.at[12]
    )
    for part in range(4):
        copies_feat[part].start()
        copies_pre[part].start()
        copies_cot[part].start()
    copy_spec.start()

    def device(d):
        return (lax.div(d, 2), lax.rem(d, 2))

    barrier = pltpu.get_barrier_semaphore()

    def signal(sem, j):
        d = jnp.bitwise_and(me + j, NDEV - 1)
        pl.semaphore_signal(sem, inc=1, device_id=device(d), device_id_type=MESH)

    for j in range(1, 8):
        signal(barrier, NDEV - j)
    for j in range(8, NDEV, 8):
        signal(barrier, j)

    def relay_entry():
        pl.semaphore_wait(barrier, 22)
        for j in range(1, 8):
            signal(relay, j)

    lane8 = lax.broadcasted_iota(jnp.int32, (8, 128), 1)

    def sums_of(source, c0):
        z0 = dot(jnp.concatenate([source[c0, 0], source[c0, 1]], axis=1), wz[...])
        z1 = dot(jnp.concatenate([source[c0 + 1, 0], source[c0 + 1, 1]], axis=1), wz[...])
        r = jnp.concatenate(
            [
                jnp.concatenate([z0[:, :128], z1[:, :128]], axis=1),
                jnp.concatenate([z0[:, 128:], z1[:, 128:]], axis=1),
            ],
            axis=0,
        )
        high, low = halves(r)
        p = dot(ty[...], high)
        y = p[:32] + p[32:] + dot(ty[0:32, :], low)
        ysc[c0] = y[:, :128]
        ysc[c0 + 1] = y[:, 128:]

    def to_messages(half, out):
        for bo in range(4):
            tiles = [ysc[half * 16 + c, bo * 8 : bo * 8 + 8, :] for c in range(16)]
            tiles = exchange_lanes(tiles, 8, lane8)
            for n in range(16):
                q, xr = n // 4, n % 4
                out[pl.ds(bo * 256 + q * 8 + xr * 2 + half, 8, stride=32), :] = tiles[n]

    def sender(src, src_at, dst, dst_at, sems):
        to_rows = pl.ds(pl.multiple_of(dst_at * 8, 8), 8)

        def send(j):
            d = jnp.bitwise_and(me + j, NDEV - 1)
            pltpu.make_async_remote_copy(
                src_ref=src.at[pl.ds(pl.multiple_of(src_at(d) * 8, 8), 8), :],
                dst_ref=dst.at[to_rows, :],
                send_sem=sems.at[0],
                recv_sem=sems.at[1],
                device_id=device(d),
                device_id_type=MESH,
            ).start()

        own = pltpu.make_async_copy(
            src.at[pl.ds(pl.multiple_of(src_at(me) * 8, 8), 8), :], dst.at[to_rows, :], sems.at[2]
        )
        return send, own

    send_h, own_h = sender(sh, lambda d: d, rh, slot, h_sems)
    send_u, own_u = sender(su, lambda d: d, ru, slot, u_sems)
    send_r, own_r = sender(
        sr, lambda d: lax.rem(d, 2) * 64 + lax.div(d, 2), rr, me, r_sems
    )

    def arrived(ref, sem):
        part = ref.at[pl.ds(0, (NDEV - 1) * 8), :]
        pltpu.make_async_copy(part, part, sem).wait()

    def slope(c0):
        if c0 % 8 == 0:
            copies_pre[c0 // 8].wait()
            copies_cot[c0 // 8].wait()
        for c in (c0, c0 + 1):
            for x in range(2):
                values = cot[c, x].astype(F32) * gelu_slope(pre[c, x].astype(F32))
                up[c, x] = values.astype(BF)

    for step in range(8):
        for c0 in (step * 4, step * 4 + 2):
            if c0 % 8 == 0:
                copies_feat[c0 // 8].wait()
            sums_of(feat, c0)
        if step == 1:
            relay_entry()
        if step % 4 == 3:
            to_messages(step // 4, su)

    pl.semaphore_wait(relay, 7)
    own_u.start()
    for j in range(1, NDEV):
        send_u(j)
    for step in range(16):
        slope(step * 2)
        sums_of(up, step * 2)
        if step % 8 == 7:
            to_messages(step // 8, sh)
    own_h.start()
    for j in range(1, NDEV):
        send_h(j)

    copy_spec.wait()

    def pack(a, carry):
        for ri in range(2):
            for j in range(2):
                parts = [
                    wraw[ri * 32 + a, pl.ds((j * 4 + k) * 32, 32), :] for k in range(4)
                ]
                wpack[ri * 2 + j, pl.ds(a, 32, stride=32), :] = jnp.concatenate(parts, axis=1)
        return carry

    lax.fori_loop(0, M, pack, 0)

    turned = lax.dot_general(
        rep[...], mix_ref[...], (((1,), (1,)), ((), ())), preferred_element_type=F32
    ).astype(BF)
    wide = lax.dot_general(
        turned, rep[...], (((1,), (1,)), ((), ())), preferred_element_type=F32
    )
    row = lax.broadcasted_iota(jnp.int32, (512, 512), 0)
    col = lax.broadcasted_iota(jnp.int32, (512, 512), 1)
    kron[...] = jnp.where(lax.rem(row, 16) == lax.rem(col, 16), wide, 0.0).astype(BF)

    def x_sums(ref, t):
        r = jnp.concatenate(
            [ref[pl.ds(t * 512, 256, stride=2), :], ref[pl.ds(t * 512 + 1, 256, stride=2), :]],
            axis=1,
        )
        high, low = halves(r)
        p = dot(tx[...], high)
        return p[:64] + p[64:] + dot(tx[0:64, :], low)

    arrived(ru, u_sems.at[1])
    own_u.wait()
    u = jnp.concatenate([x_sums(ru, 0), x_sums(ru, 1)], axis=0)
    u_high, u_low = halves(u)
    p = dot(jnp.concatenate([u_high, u_low], axis=0), order[...])
    u = p[:128] + p[128:]

    arrived(rh, h_sems.at[1])
    own_h.wait()
    lane256 = lax.broadcasted_iota(jnp.int32, (1, 256), 1)
    single = jnp.logical_and(lax.rem(lane256, 8) == 0, quarter == 0)
    hermit = jnp.where(single, 1.0, 2.0).astype(F32)
    h = jnp.concatenate([x_sums(rh, 0), x_sums(rh, 1)], axis=0) * hermit
    h_high, h_low = halves(h)
    h_both = jnp.concatenate([h_high, h_low], axis=0)

    def mode_sum(o, sums):
        picked = jnp.where(lax.div(lane256, 8) == o, h_both, jnp.zeros_like(h_both))
        p = dot(picked, spread[...])
        spread_h = p[:128] + p[128:]
        hx[o] = spread_h
        rows = pl.ds(pl.multiple_of(o * 32, 32), 32)
        later = []
        for j in range(2):
            w_real = wpack[j, rows, :]
            w_imag = wpack[2 + j, rows, :]
            for t in range(2):
                h_real = spread_h[t * 64 : t * 64 + 32, j * 128 : j * 128 + 128]
                h_imag = spread_h[t * 64 + 32 : t * 64 + 64, j * 128 : j * 128 + 128]
                d_real, d_imag = sums[(j * 2 + t) * 2], sums[(j * 2 + t) * 2 + 1]
                later.append(d_real + w_real * h_real + w_imag * h_imag)
                later.append(d_imag + w_real * h_imag - w_imag * h_real)
        return tuple(later)

    zero = jnp.zeros((32, 128), F32)
    sums = lax.fori_loop(0, C, mode_sum, (zero,) * 8, unroll=4)
    for t in range(2):
        left = jnp.concatenate([sums[t * 2], sums[t * 2 + 1]], axis=0)
        right = jnp.concatenate([sums[4 + t * 2], sums[5 + t * 2]], axis=0)
        high, low = halves(jnp.concatenate([left, right], axis=1))
        x_syn = dot(xs[...], jnp.concatenate([high, low, high], axis=0))
        sr[pl.ds(t * 512, 256, stride=2), :] = x_syn[:, :128]
        sr[pl.ds(t * 512 + 1, 256, stride=2), :] = x_syn[:, 128:]
    own_r.start()
    def mixing(yb):
        y0 = yb * 16
        for x in range(2):
            block = up[:, x, y0 : y0 + 16, :].reshape(512, 128)
            mixed[:, x, y0 : y0 + 16, :] = dot(kron[...], block).reshape(C, 16, 128)

    for j in range(1, NDEV):
        send_r(j)
    for yb in range(8):
        mixing(yb)


    for j in range(2):
        lanes = slice(j * 128, j * 128 + 128)
        for ah in range(2):
            u_parts = [u[r * 32 + ah * 16 : r * 32 + ah * 16 + 16, lanes] for r in range(4)]

            def outer(o, carry):
                hs = [hx[o, r * 32 + ah * 16 : r * 32 + ah * 16 + 16, lanes] for r in range(4)]
                real = hs[0] * u_parts[0] + hs[1] * u_parts[1] + hs[2] * u_parts[2] + hs[3] * u_parts[3]
                imag = hs[1] * u_parts[0] - hs[0] * u_parts[1] + hs[3] * u_parts[2] - hs[2] * u_parts[3]
                rows = pl.ds(pl.multiple_of(o * 32 + ah * 16, 16), 16)
                gpack[j, rows, :] = real
                gpack[2 + j, rows, :] = imag
                return carry

            lax.fori_loop(0, C, outer, 0)

    def unpack(a, carry):
        for ri in range(2):
            for j in range(2):
                tile = gpack[ri * 2 + j, pl.ds(a, 32, stride=32), :]
                for k in range(4):
                    gout[ri * 32 + a, pl.ds((j * 4 + k) * 32, 32), :] = tile[:, k * 32 : k * 32 + 32]
        return carry

    lax.fori_loop(0, M, unpack, 0)

    arrived(rr, r_sems.at[1])
    own_r.wait()
    arrived(sh, h_sems.at[0])
    arrived(su, u_sems.at[0])
    arrived(sr, r_sems.at[0])


def synthesis(rr, mixed, gout, ys, zh, zl, field_hbm, grad_hbm, fout, sems):
    lane8 = lax.broadcasted_iota(jnp.int32, (8, 128), 1)
    copy_grad = pltpu.make_async_copy(gout, grad_hbm, sems.at[8])
    copy_grad.start()
    tiles = [[[None] * 8 for _ in range(8)] for _ in range(2)]
    for x in range(2):
        for ri in range(2):
            for bo in range(4):
                loaded = [
                    rr[pl.ds(bo * 256 + (n // 2) * 8 + x * 4 + ri * 2 + n % 2, 8, stride=32), :]
                    for n in range(8)
                ]
                for ig, tile in enumerate(exchange_lanes(loaded, 4, lane8)):
                    tiles[x][ig][ri * 4 + bo] = tile
    copies = []
    for ig in range(8):
        for x in range(2):
            high, low = halves(jnp.concatenate(tiles[x][ig], axis=0))
            y_syn = dot(ys[...], jnp.concatenate([high, low, high], axis=0))
            high, low = halves(jnp.concatenate([y_syn[:128], y_syn[128:]], axis=1))
            z_syn = dot(high, zh[...]) + dot(low, zh[...]) + dot(high, zl[...])
            for i in range(4):
                total = mixed[ig * 4 + i, x] + z_syn[:, i * 128 : i * 128 + 128]
                fout[ig * 4 + i, x] = total.astype(BF)
        rows = pl.ds(ig * 4, 4)
        copies.append(pltpu.make_async_copy(fout.at[rows], field_hbm.at[rows], sems.at[ig]))
        copies[-1].start()
    for copy in copies:
        copy.wait()
    copy_grad.wait()


def shards(features, pre_act, cotangent, mix_weight, spec_weight):
    planes = (C, 2, G, G)
    consts = tables()
    anywhere = pl.BlockSpec(memory_space=pl.ANY)
    inside = pl.BlockSpec(memory_space=pltpu.VMEM)
    message = pltpu.VMEM((NDEV * 8, 128), F32)
    grad_shape = (64, 256, 32)
    first = ("wz", "ty", "tx", "xs", "spread", "order", "rep")
    returned, mixed, grad = pl.pallas_call(
        gather,
        out_shape=(
            pltpu.VMEM((NDEV * 8, 128), F32),
            pltpu.VMEM(planes, F32),
            pltpu.VMEM(grad_shape, F32),
        ),
        in_specs=[anywhere] * 3 + [inside] + [anywhere] + [inside] * len(first),
        out_specs=(inside, inside, inside),
        scratch_shapes=[
            pltpu.VMEM(planes, BF),
            pltpu.VMEM(planes, BF),
            pltpu.VMEM(planes, BF),
            pltpu.VMEM(grad_shape, F32),
            pltpu.VMEM(planes, BF),
            pltpu.VMEM((4, 1024, 128), F32),
            pltpu.VMEM((C, 32, 128), F32),
            message, message, message, message, message,
            pltpu.VMEM((C, 128, 256), F32),
            pltpu.VMEM((4, 1024, 128), F32),
            pltpu.VMEM((512, 512), BF),
            pltpu.SemaphoreType.DMA((13,)),
            pltpu.SemaphoreType.DMA((3,)),
            pltpu.SemaphoreType.DMA((3,)),
            pltpu.SemaphoreType.DMA((3,)),
            pltpu.SemaphoreType.REGULAR,
        ],
        compiler_params=pltpu.CompilerParams(
            collective_id=0, has_side_effects=True, vmem_limit_bytes=44 * 2**20
        ),
    )(
        features.reshape(planes),
        pre_act.reshape(planes),
        cotangent.reshape(planes),
        mix_weight,
        spec_weight.reshape(64, 512, 32),
        *[jnp.asarray(consts[name]) for name in first],
    )
    second = ("ys", "zh", "zl")
    field, grad = pl.pallas_call(
        synthesis,
        out_shape=(
            jax.ShapeDtypeStruct(planes, BF),
            jax.ShapeDtypeStruct(grad_shape, F32),
        ),
        in_specs=[inside] * (3 + len(second)),
        out_specs=(anywhere, anywhere),
        scratch_shapes=[
            pltpu.VMEM(planes, BF),
            pltpu.SemaphoreType.DMA((9,)),
        ],
        compiler_params=pltpu.CompilerParams(vmem_limit_bytes=40 * 2**20),
    )(returned, mixed, grad, *[jnp.asarray(consts[name]) for name in second])
    return field.reshape(features.shape), grad.reshape(2, M, 8, C, C)


def solution(mesh):
    placed = P("samp", None, "space", None, None)
    return jax.shard_map(
        shards,
        mesh=mesh,
        in_specs=(placed, placed, placed, P(), P(None, None, "space", None, None)),
        out_specs=(placed, P(None, None, ("space", "samp"), None, None)),
        check_vma=False,
    )
```

```python
import math

import jax
import jax.numpy as jnp
import ml_dtypes
import numpy as np
from jax import lax
from jax.experimental import pallas as pl
from jax.experimental.pallas import tpu as pltpu
from jax.sharding import PartitionSpec as P

MESH = pl.DeviceIdType.MESH
BF = jnp.bfloat16
F32 = jnp.float32
C = 32
M = 32
G = 128
NX = 128
NDEV = 128
NRM = 1.0 / math.sqrt(NX * G * G)


def split_np(values):
    high = values.astype(ml_dtypes.bfloat16)
    low = (values - high.astype(np.float64)).astype(ml_dtypes.bfloat16)
    return high, low


def tables():
    freq = np.arange(M) - M // 2
    pos = np.arange(G)

    def waves(positions, freqs):
        angles = np.mod(positions[:, None] * freqs[None, :], G) * (2.0 * math.pi / G)
        return np.cos(angles), np.sin(angles)

    cos_z, sin_z = waves(pos, np.arange(M))
    cos_c, sin_c = waves(pos, freq)
    cz = cos_z.reshape(G, 4, 8)
    sz = sin_z.reshape(G, 4, 8)
    wz = np.zeros((2, G, 2, 4, 2, 2, 8))
    for x in range(2):
        wz[x, :, 0, :, x, 0] = cz
        wz[x, :, 0, :, x, 1] = -sz
        wz[x, :, 1, :, x, 0] = -sz
        wz[x, :, 1, :, x, 1] = -cz
    wz = wz.reshape(256, 256).astype(ml_dtypes.bfloat16)
    ty = np.concatenate([cos_c.T, sin_c.T], axis=1)
    ty = np.concatenate(split_np(ty), axis=0)
    tx = np.zeros((2, M, NX, 2))
    tx[0, :, :, 0] = cos_c.T
    tx[0, :, :, 1] = sin_c.T
    tx[1, :, :, 0] = -sin_c.T
    tx[1, :, :, 1] = cos_c.T
    tx = tx.reshape(64, 256)
    txh = np.concatenate(split_np(tx * NRM), axis=0)
    xh, xl = split_np(tx.T.copy())
    xs = np.concatenate([xh, xh, xl], axis=1)
    ys = np.zeros((2, G, 2, M))
    ys[0, :, 0] = cos_c
    ys[0, :, 1] = -sin_c
    ys[1, :, 0] = sin_c
    ys[1, :, 1] = cos_c
    yh, yl = split_np(ys.reshape(256, 64) * NRM)
    ys = np.concatenate([yh, yh, yl], axis=1)
    zs = np.zeros((2, 4, 8, 4, 4, G))
    ck = cos_z.T.reshape(8, 4, G).transpose(1, 0, 2)
    sk = sin_z.T.reshape(8, 4, G).transpose(1, 0, 2)
    for i in range(4):
        zs[0, :, :, i, i] = ck
        zs[1, :, :, i, i] = -sk
    zh, zl = split_np(zs.reshape(256, 512))
    eye8 = np.eye(8)
    spread = np.broadcast_to(eye8[None, :, :, None], (C, 8, 8, C)).reshape(256, 256)
    order = np.einsum("cd,kl->ckld", np.eye(C), eye8).reshape(256, 256)
    rep = np.repeat(np.eye(C), 16, axis=0)
    names = dict(wz=wz, ty=ty, tx=txh, xs=xs, ys=ys, zh=zh, zl=zl, spread=spread, order=order, rep=rep)
    return {name: np.ascontiguousarray(v).astype(ml_dtypes.bfloat16) for name, v in names.items()}


def halves(values):
    high = values.astype(BF)
    return high, (values - high.astype(F32)).astype(BF)


def dot(left, right):
    return jnp.dot(left, right, preferred_element_type=F32)


def gelu_slope(values):
    return 0.5 * (1.0 + lax.erf(values * 0.7071067811865476)) + values * (
        jnp.exp(-0.5 * values * values) * 0.3989422804014327
    )


def exchange_lanes(tiles, unit, lane):
    tiles = list(tiles)
    step = 1
    while step < len(tiles):
        keep = (lane // (unit * step)) % 2 == 0
        for i in range(len(tiles)):
            if i & step:
                continue
            low, high = tiles[i], tiles[i | step]
            tiles[i] = jnp.where(keep, low, pltpu.roll(high, unit * step, 1))
            tiles[i | step] = jnp.where(keep, pltpu.roll(low, 128 - unit * step, 1), high)
        step *= 2
    return tiles


def gather(
    feat_hbm, pre_hbm, cot_hbm, mix_hbm, spec_hbm,
    wz_hbm, ty_hbm, tx_hbm, xs_hbm, spread_hbm, order_hbm, rep_hbm,
    rr, mixed, gout,
    feat, pre, cot, wraw, up, wpack, ysc, sh, su, rh, ru, sr, hx, gpack, kron,
    mix_ref, wz, ty, tx, xs, spread, order, rep,
    in_sems, table_sems, h_sems, u_sems, r_sems, relay,
):
    space = lax.axis_index("space")
    samp = lax.axis_index("samp")
    me = space * 2 + samp
    slot = samp * 64 + space
    quarter = lax.rem(me, 4)

    def parts_of(hbm, vmem, first):
        rows = [pl.ds(part * 8, 8) for part in range(4)]
        return [
            pltpu.make_async_copy(hbm.at[r], vmem.at[r], in_sems.at[first + part])
            for part, r in enumerate(rows)
        ]

    copies_pre = parts_of(pre_hbm, pre, 0)
    copies_cot = parts_of(cot_hbm, cot, 4)
    copies_feat = parts_of(feat_hbm, feat, 8)
    copy_spec = pltpu.make_async_copy(
        spec_hbm.at[:, pl.ds(samp * 256, 256), :], wraw, in_sems.at[12]
    )
    table_pairs = (
        (wz_hbm, wz), (ty_hbm, ty), (mix_hbm, mix_ref), (tx_hbm, tx),
        (xs_hbm, xs), (spread_hbm, spread), (order_hbm, order), (rep_hbm, rep),
    )
    copies_table = [
        pltpu.make_async_copy(hbm, vmem, table_sems.at[i])
        for i, (hbm, vmem) in enumerate(table_pairs)
    ]
    copies_feat[0].start()
    copies_table[0].start()
    copies_table[1].start()
    for part in range(4):
        if part:
            copies_feat[part].start()
        copies_pre[part].start()
        copies_cot[part].start()
    for copy in copies_table[2:]:
        copy.start()
    copy_spec.start()

    def device(d):
        return (lax.div(d, 2), lax.rem(d, 2))

    barrier = pltpu.get_barrier_semaphore()

    def signal(sem, j):
        d = jnp.bitwise_and(me + j, NDEV - 1)
        pl.semaphore_signal(sem, inc=1, device_id=device(d), device_id_type=MESH)

    for j in range(1, 8):
        signal(barrier, NDEV - j)
    for j in range(8, NDEV, 8):
        signal(barrier, j)

    def relay_entry():
        pl.semaphore_wait(barrier, 22)
        for j in range(1, 8):
            signal(relay, j)

    lane8 = lax.broadcasted_iota(jnp.int32, (8, 128), 1)

    def sums_of(source, c0):
        z0 = dot(jnp.concatenate([source[c0, 0], source[c0, 1]], axis=1), wz[...])
        z1 = dot(jnp.concatenate([source[c0 + 1, 0], source[c0 + 1, 1]], axis=1), wz[...])
        r = jnp.concatenate(
            [
                jnp.concatenate([z0[:, :128], z1[:, :128]], axis=1),
                jnp.concatenate([z0[:, 128:], z1[:, 128:]], axis=1),
            ],
            axis=0,
        )
        high, low = halves(r)
        p = dot(ty[...], high)
        y = p[:32] + p[32:] + dot(ty[0:32, :], low)
        ysc[c0] = y[:, :128]
        ysc[c0 + 1] = y[:, 128:]

    def to_messages(half, out):
        for bo in range(4):
            tiles = [ysc[half * 16 + c, bo * 8 : bo * 8 + 8, :] for c in range(16)]
            tiles = exchange_lanes(tiles, 8, lane8)
            for n in range(16):
                q, xr = n // 4, n % 4
                out[pl.ds(bo * 256 + q * 8 + xr * 2 + half, 8, stride=32), :] = tiles[n]

    def sender(src, src_at, dst, dst_at, sems):
        to_rows = pl.ds(pl.multiple_of(dst_at * 8, 8), 8)

        def send(j):
            d = jnp.bitwise_and(me + j, NDEV - 1)
            pltpu.make_async_remote_copy(
                src_ref=src.at[pl.ds(pl.multiple_of(src_at(d) * 8, 8), 8), :],
                dst_ref=dst.at[to_rows, :],
                send_sem=sems.at[0],
                recv_sem=sems.at[1],
                device_id=device(d),
                device_id_type=MESH,
            ).start()

        own = pltpu.make_async_copy(
            src.at[pl.ds(pl.multiple_of(src_at(me) * 8, 8), 8), :], dst.at[to_rows, :], sems.at[2]
        )
        return send, own

    send_h, own_h = sender(sh, lambda d: d, rh, slot, h_sems)
    send_u, own_u = sender(su, lambda d: d, ru, slot, u_sems)
    send_r, own_r = sender(
        sr, lambda d: lax.rem(d, 2) * 64 + lax.div(d, 2), rr, me, r_sems
    )

    def arrived(ref, sem):
        part = ref.at[pl.ds(0, (NDEV - 1) * 8), :]
        pltpu.make_async_copy(part, part, sem).wait()

    def slope(c0):
        if c0 % 8 == 0:
            copies_pre[c0 // 8].wait()
            copies_cot[c0 // 8].wait()
        for c in (c0, c0 + 1):
            for x in range(2):
                values = cot[c, x].astype(F32) * gelu_slope(pre[c, x].astype(F32))
                up[c, x] = values.astype(BF)

    copies_table[0].wait()
    copies_table[1].wait()
    for step in range(8):
        for c0 in (step * 4, step * 4 + 2):
            if c0 % 8 == 0:
                copies_feat[c0 // 8].wait()
            sums_of(feat, c0)
        if step == 1:
            relay_entry()
        if step % 4 == 3:
            to_messages(step // 4, su)

    pl.semaphore_wait(relay, 7)
    own_u.start()
    for j in range(1, NDEV):
        send_u(j)
    for step in range(16):
        slope(step * 2)
        sums_of(up, step * 2)
        if step % 8 == 7:
            to_messages(step // 8, sh)
    own_h.start()
    for j in range(1, NDEV):
        send_h(j)

    for copy in copies_table[2:]:
        copy.wait()
    copy_spec.wait()

    def pack(a, carry):
        for ri in range(2):
            for j in range(2):
                parts = [
                    wraw[ri * 32 + a, pl.ds((j * 4 + k) * 32, 32), :] for k in range(4)
                ]
                wpack[ri * 2 + j, pl.ds(a, 32, stride=32), :] = jnp.concatenate(parts, axis=1)
        return carry

    lax.fori_loop(0, M, pack, 0)

    turned = lax.dot_general(
        rep[...], mix_ref[...], (((1,), (1,)), ((), ())), preferred_element_type=F32
    ).astype(BF)
    wide = lax.dot_general(
        turned, rep[...], (((1,), (1,)), ((), ())), preferred_element_type=F32
    )
    row = lax.broadcasted_iota(jnp.int32, (512, 512), 0)
    col = lax.broadcasted_iota(jnp.int32, (512, 512), 1)
    kron[...] = jnp.where(lax.rem(row, 16) == lax.rem(col, 16), wide, 0.0).astype(BF)

    def x_sums(ref, t):
        r = jnp.concatenate(
            [ref[pl.ds(t * 512, 256, stride=2), :], ref[pl.ds(t * 512 + 1, 256, stride=2), :]],
            axis=1,
        )
        high, low = halves(r)
        p = dot(tx[...], high)
        return p[:64] + p[64:] + dot(tx[0:64, :], low)

    arrived(ru, u_sems.at[1])
    own_u.wait()
    u = jnp.concatenate([x_sums(ru, 0), x_sums(ru, 1)], axis=0)
    u_high, u_low = halves(u)
    p = dot(jnp.concatenate([u_high, u_low], axis=0), order[...])
    u = p[:128] + p[128:]

    arrived(rh, h_sems.at[1])
    own_h.wait()
    lane256 = lax.broadcasted_iota(jnp.int32, (1, 256), 1)
    single = jnp.logical_and(lax.rem(lane256, 8) == 0, quarter == 0)
    hermit = jnp.where(single, 1.0, 2.0).astype(F32)
    h = jnp.concatenate([x_sums(rh, 0), x_sums(rh, 1)], axis=0) * hermit
    h_high, h_low = halves(h)
    h_both = h_high

    def mode_sum(o, sums):
        picked = jnp.where(lax.div(lane256, 8) == o, h_both, jnp.zeros_like(h_both))
        spread_h = dot(picked, spread[...])
        hx[o] = spread_h
        rows = pl.ds(pl.multiple_of(o * 32, 32), 32)
        later = []
        for j in range(2):
            w_real = wpack[j, rows, :]
            w_imag = wpack[2 + j, rows, :]
            for t in range(2):
                h_real = spread_h[t * 64 : t * 64 + 32, j * 128 : j * 128 + 128]
                h_imag = spread_h[t * 64 + 32 : t * 64 + 64, j * 128 : j * 128 + 128]
                d_real, d_imag = sums[(j * 2 + t) * 2], sums[(j * 2 + t) * 2 + 1]
                later.append(d_real + w_real * h_real + w_imag * h_imag)
                later.append(d_imag + w_real * h_imag - w_imag * h_real)
        return tuple(later)

    zero = jnp.zeros((32, 128), F32)
    sums = lax.fori_loop(0, C, mode_sum, (zero,) * 8, unroll=4)
    for t in range(2):
        left = jnp.concatenate([sums[t * 2], sums[t * 2 + 1]], axis=0)
        right = jnp.concatenate([sums[4 + t * 2], sums[5 + t * 2]], axis=0)
        high, low = halves(jnp.concatenate([left, right], axis=1))
        x_syn = dot(xs[...], jnp.concatenate([high, low, high], axis=0))
        sr[pl.ds(t * 512, 256, stride=2), :] = x_syn[:, :128]
        sr[pl.ds(t * 512 + 1, 256, stride=2), :] = x_syn[:, 128:]
    own_r.start()
    def mixing(yb):
        y0 = yb * 16
        for x in range(2):
            block = up[:, x, y0 : y0 + 16, :].reshape(512, 128)
            mixed[:, x, y0 : y0 + 16, :] = dot(kron[...], block).reshape(C, 16, 128)

    for j in range(1, NDEV):
        send_r(j)
    for yb in range(8):
        mixing(yb)


    for j in range(2):
        lanes = slice(j * 128, j * 128 + 128)
        for ah in range(2):
            u_parts = [u[r * 32 + ah * 16 : r * 32 + ah * 16 + 16, lanes] for r in range(4)]

            def outer(o, carry):
                hs = [hx[o, r * 32 + ah * 16 : r * 32 + ah * 16 + 16, lanes] for r in range(4)]
                real = hs[0] * u_parts[0] + hs[1] * u_parts[1] + hs[2] * u_parts[2] + hs[3] * u_parts[3]
                imag = hs[1] * u_parts[0] - hs[0] * u_parts[1] + hs[3] * u_parts[2] - hs[2] * u_parts[3]
                rows = pl.ds(pl.multiple_of(o * 32 + ah * 16, 16), 16)
                gpack[j, rows, :] = real
                gpack[2 + j, rows, :] = imag
                return carry

            lax.fori_loop(0, C, outer, 0)

    def unpack(a, carry):
        for ri in range(2):
            for j in range(2):
                tile = gpack[ri * 2 + j, pl.ds(a, 32, stride=32), :]
                for k in range(4):
                    gout[ri * 32 + a, pl.ds((j * 4 + k) * 32, 32), :] = tile[:, k * 32 : k * 32 + 32]
        return carry

    lax.fori_loop(0, M, unpack, 0)

    arrived(rr, r_sems.at[1])
    own_r.wait()
    arrived(sh, h_sems.at[0])
    arrived(su, u_sems.at[0])
    arrived(sr, r_sems.at[0])


def synthesis(rr, mixed, gout, ys, zh, zl, field_hbm, grad_hbm, fout, sems):
    lane8 = lax.broadcasted_iota(jnp.int32, (8, 128), 1)
    copy_grad = pltpu.make_async_copy(gout, grad_hbm, sems.at[8])
    copy_grad.start()
    tiles = [[[None] * 8 for _ in range(8)] for _ in range(2)]
    for x in range(2):
        for ri in range(2):
            for bo in range(4):
                loaded = [
                    rr[pl.ds(bo * 256 + (n // 2) * 8 + x * 4 + ri * 2 + n % 2, 8, stride=32), :]
                    for n in range(8)
                ]
                for ig, tile in enumerate(exchange_lanes(loaded, 4, lane8)):
                    tiles[x][ig][ri * 4 + bo] = tile
    copies = []
    for ig in range(8):
        for x in range(2):
            high, low = halves(jnp.concatenate(tiles[x][ig], axis=0))
            y_syn = dot(ys[...], jnp.concatenate([high, low, high], axis=0))
            high, low = halves(jnp.concatenate([y_syn[:128], y_syn[128:]], axis=1))
            z_syn = dot(high, zh[...]) + dot(low, zh[...]) + dot(high, zl[...])
            for i in range(4):
                total = mixed[ig * 4 + i, x] + z_syn[:, i * 128 : i * 128 + 128]
                fout[ig * 4 + i, x] = total.astype(BF)
        rows = pl.ds(ig * 4, 4)
        copies.append(pltpu.make_async_copy(fout.at[rows], field_hbm.at[rows], sems.at[ig]))
        copies[-1].start()
    for copy in copies:
        copy.wait()
    copy_grad.wait()


def shards(features, pre_act, cotangent, mix_weight, spec_weight):
    planes = (C, 2, G, G)
    consts = tables()
    anywhere = pl.BlockSpec(memory_space=pl.ANY)
    inside = pl.BlockSpec(memory_space=pltpu.VMEM)
    message = pltpu.VMEM((NDEV * 8, 128), F32)
    grad_shape = (64, 256, 32)
    first = ("wz", "ty", "tx", "xs", "spread", "order", "rep")
    returned, mixed, grad = pl.pallas_call(
        gather,
        out_shape=(
            pltpu.VMEM((NDEV * 8, 128), F32),
            pltpu.VMEM(planes, F32),
            pltpu.VMEM(grad_shape, F32),
        ),
        in_specs=[anywhere] * (5 + len(first)),
        out_specs=(inside, inside, inside),
        scratch_shapes=[
            pltpu.VMEM(planes, BF),
            pltpu.VMEM(planes, BF),
            pltpu.VMEM(planes, BF),
            pltpu.VMEM(grad_shape, F32),
            pltpu.VMEM(planes, BF),
            pltpu.VMEM((4, 1024, 128), F32),
            pltpu.VMEM((C, 32, 128), F32),
            message, message, message, message, message,
            pltpu.VMEM((C, 128, 256), F32),
            pltpu.VMEM((4, 1024, 128), F32),
            pltpu.VMEM((512, 512), BF),
            pltpu.VMEM((C, C), BF),
            *[pltpu.VMEM(consts[name].shape, BF) for name in first],
            pltpu.SemaphoreType.DMA((13,)),
            pltpu.SemaphoreType.DMA((8,)),
            pltpu.SemaphoreType.DMA((3,)),
            pltpu.SemaphoreType.DMA((3,)),
            pltpu.SemaphoreType.DMA((3,)),
            pltpu.SemaphoreType.REGULAR,
        ],
        compiler_params=pltpu.CompilerParams(
            collective_id=0, has_side_effects=True, vmem_limit_bytes=44 * 2**20
        ),
    )(
        features.reshape(planes),
        pre_act.reshape(planes),
        cotangent.reshape(planes),
        mix_weight,
        spec_weight.reshape(64, 512, 32),
        *[jnp.asarray(consts[name]) for name in first],
    )
    second = ("ys", "zh", "zl")
    field, grad = pl.pallas_call(
        synthesis,
        out_shape=(
            jax.ShapeDtypeStruct(planes, BF),
            jax.ShapeDtypeStruct(grad_shape, F32),
        ),
        in_specs=[inside] * (3 + len(second)),
        out_specs=(anywhere, anywhere),
        scratch_shapes=[
            pltpu.VMEM(planes, BF),
            pltpu.SemaphoreType.DMA((9,)),
        ],
        compiler_params=pltpu.CompilerParams(vmem_limit_bytes=40 * 2**20),
    )(returned, mixed, grad, *[jnp.asarray(consts[name]) for name in second])
    return field.reshape(features.shape), grad.reshape(2, M, 8, C, C)


def solution(mesh):
    placed = P("samp", None, "space", None, None)
    return jax.shard_map(
        shards,
        mesh=mesh,
        in_specs=(placed, placed, placed, P(), P(None, None, "space", None, None)),
        out_specs=(placed, P(None, None, ("space", "samp"), None, None)),
        check_vma=False,
    )
```
